256 devices in a mesh: replica: 16 (over y, z_lo, core), fsdp: 16 (over x, z_hi).
Axes of the slice: x: 4, y: 4, z: 8 (z_hi: 4, z_lo: 2; z = z_hi * 2 + z_lo), core: 2. Of those that a mesh axis runs over, the one named last changes fastest.
Arguments:
- activations: bfloat16 [16, 10240, 4608], P('replica', 'fsdp'), may hold values from -6 to 6
- teacher: bfloat16 [16, 10240, 1024], P('replica', 'fsdp'), may hold values from -6 to 6
- weights: float32 [16, 4608, 1024], P('replica', 'fsdp'), may hold values from -6 to 6
- first_moment: float32 [16, 4608, 1024], P('replica', 'fsdp'), may hold values from -0.001953125 to 0.001953125
- second_moment: float32 [16, 4608, 1024], P('replica', 'fsdp'), may hold values from 2.1192763e-10 to 2.1192763e-08
- anchor: float32 [4, 4608, 256], P(None, 'fsdp', 'replica'), may hold values from -6 to 6
- momentum: float32 [4, 4608, 256], P(None, 'fsdp', 'replica'), may hold values from -6 to 6
- fragment: int32 [1], replicated, may hold values from 0 to 255
Outputs:
- new_weights: float32 [16, 4608, 1024], P('replica', 'fsdp')
- new_anchor: float32 [4, 4608, 256], P(None, 'fsdp', 'replica')
- new_momentum: float32 [4, 4608, 256], P(None, 'fsdp', 'replica')
The draws below stay inside these ranges and needn't reach their ends.
All inputs are finite; a program needn't handle non-finite values.
Results may differ from the reference program's by a relative error of at most 0.007.
Values may be sent and summed in bfloat16 or wider, within the bound.
A program may use at most 128 MiB of HBM per device.

```python
import math
import jax
import jax.numpy as jnp
from jax import lax

D = 4608
R = 1024
FRAGS = 4
WINDOWS = 256
TOK_DEV = 640
FW = 256
BATCH = 10240
REPLICAS = 16
N_REPLICA = 16


def steps_of(own_key, dims, shards, least, high):
    def one(axis_at, parts):
        draws = jax.random.uniform(jax.random.fold_in(jax.random.fold_in(own_key, 6), axis_at), (parts,), jnp.float32, least / len(shards), high / len(shards))
        return jnp.repeat(jnp.exp(draws), dims[axis_at] // parts).reshape((-1,) + (1,) * (len(dims) - axis_at - 1))

    level = one(*shards[0])
    for cut in shards[1:]:
        level = level * one(*cut)
    return level


def centred(rng, dims, spread, most, shards=(), dtype=jnp.bfloat16):
    array = spread * jax.random.normal(rng, dims, jnp.float32)
    if shards:
        array = array * steps_of(rng, dims, shards, -0.22, 0.18)
    return jnp.clip(array, -most, most).astype(dtype)


def setup_inputs(seed: int = 0) -> dict:
    splits = jax.random.split(jax.random.key(seed), 9)
    activations = centred(splits[0], (REPLICAS, BATCH, D), 1.0, 6.0, ((0, 16), (1, 16)))
    teacher = centred(splits[1], (REPLICAS, BATCH, R), 1.0, 6.0, ((0, 16), (1, 16)))
    weights = centred(splits[2], (REPLICAS, D, R), 1.0, 6.0, ((0, 16), (1, 16)), jnp.float32)
    first_moment = centred(splits[3], (REPLICAS, D, R), (1.0 / (BATCH * D) ** 0.5), 0.001953125, ((0, 16), (1, 16)), jnp.float32)
    second_moment = jnp.clip(jnp.exp(math.log(2.119276309997531e-08) - 4.6051702 * jax.random.uniform(splits[4], (REPLICAS, D, R), jnp.float32) ** steps_of(splits[4], (REPLICAS, D, R), ((0, 16), (1, 16)), -0.2, 0.2)), 2.1192762822419553e-10, 2.119276309997531e-08)
    anchor = centred(splits[5], (FRAGS, D, FW), 1.0, 6.0, ((1, 16), (2, 16)), jnp.float32)
    momentum = centred(splits[6], (FRAGS, D, FW), 0.5, 6.0, ((1, 16), (2, 16)), jnp.float32)
    fragment = jax.random.randint(splits[7], (1,), 0, WINDOWS).astype(jnp.int32)
    return {"activations": activations, "teacher": teacher, "weights": weights, "first_moment": first_moment, "second_moment": second_moment, "anchor": anchor, "momentum": momentum, "fragment": fragment}


def reference(activations, teacher, weights, first_moment, second_moment, anchor, momentum, fragment):
    scale = 1.0 / math.sqrt(D)
    window = fragment[0].astype(jnp.int32)
    index = jnp.remainder(window, FRAGS).astype(jnp.int32)
    outer_rate = 0.4 + 0.6 * window.astype(jnp.float32) / WINDOWS
    blocks = BATCH // TOK_DEV

    def one_replica(items):
        inputs, target, master, moment_a, moment_b = items
        low = master.astype(jnp.bfloat16)
        values = jnp.dot(inputs, low, preferred_element_type=jnp.float32) * scale
        error = ((values - target.astype(jnp.float32)) / BATCH).astype(jnp.bfloat16)
        in_blocks = inputs.reshape(blocks, TOK_DEV, inputs.shape[1])
        err_blocks = error.reshape(blocks, TOK_DEV, error.shape[1])

        def add_block(total, pair):
            part_in, part_err = pair
            partial_value = jnp.dot(part_in.T, part_err, preferred_element_type=jnp.float32).astype(jnp.bfloat16)
            partial_value = lax.optimization_barrier(partial_value)
            return (total + partial_value.astype(jnp.float32), None)
        summed, _ = lax.scan(add_block, jnp.zeros(master.shape, jnp.float32), (in_blocks, err_blocks))
        grad = summed * scale
        moment1 = 0.9 * moment_a + 0.1 * grad
        moment2 = 0.95 * moment_b + 0.05 * grad * grad
        return master - 0.25 * (moment1 / (jnp.sqrt(moment2) + 1e-08) + 0.1 * master)
    stepped = lax.map(one_replica, (activations, teacher, weights, first_moment, second_moment))
    start_col = index * FW
    old_block = lax.dynamic_slice_in_dim(weights, start_col, FW, 2)
    own_anchor = lax.dynamic_index_in_dim(anchor, index, 0, keepdims=False)
    own_moment = lax.dynamic_index_in_dim(momentum, index, 0, keepdims=False)
    outer_grad = lax.optimization_barrier(jnp.sum(own_anchor[None] - old_block, axis=0)) / N_REPLICA
    moment_next = 0.9 * own_moment + outer_grad
    anchor_next = own_anchor - outer_rate * (outer_grad + 0.9 * moment_next)
    new_momentum = lax.dynamic_update_index_in_dim(momentum, moment_next, index, 0)
    new_anchor = lax.dynamic_update_index_in_dim(anchor, anchor_next, index, 0)
    mixed = 0.5 * anchor_next[None] + 0.5 * lax.dynamic_slice_in_dim(stepped, start_col, FW, 2)
    new_weights = lax.dynamic_update_slice_in_dim(stepped, mixed, start_col, 2)
    return (new_weights, new_anchor, new_momentum)
```

```python
import functools
import math

import jax
import jax.numpy as jnp
from jax import lax
from jax.experimental import pallas as pl
from jax.experimental.pallas import tpu as pltpu
from jax.sharding import PartitionSpec as P

FRAGS = 4
WINDOWS = 256
SIDE = 4
CHUNKS = 4
ROWS_A = 224
LANES = 384
MESH = pl.DeviceIdType.MESH
F32 = jnp.float32
BF16 = jnp.bfloat16


def kernel(
    batch,
    frag_ref,
    act_hbm,
    tgt_hbm,
    w_hbm,
    m1_hbm,
    m2_hbm,
    anc_ref,
    mom_ref,
    nw_hbm,
    na_ref,
    nm_ref,
    act,
    act_t,
    tgt,
    w,
    m1,
    m2,
    nw,
    wf,
    pt,
    err,
    acc,
    rxh,
    rxf,
    rzh,
    rzf,
    bzh,
    bzf,
    bxh,
    bxf,
    tall,
    old_t,
    anc_t,
    anc_full,
    got,
    in_sem,
    out_sem,
    ssem,
    rsem,
    osend,
    orecv,
):
    nc, rows, cw = wf.shape[0], wf.shape[3], wf.shape[4]
    ra, rb = ROWS_A, rows - ROWS_A
    ha, hb = ra // 2, rb // 2
    depth = act.shape[1]
    scale = 1.0 / math.sqrt(depth)
    group = SIDE * rows

    me = lax.axis_index("fsdp")
    rep = lax.axis_index("replica")
    replicas = lax.axis_size("replica")
    x, z = lax.div(me, SIDE), lax.rem(me, SIDE)
    xp, xm, x2 = (lax.rem(x + k, SIDE) for k in (1, 3, 2))
    zp, zm, z2 = (lax.rem(z + k, SIDE) for k in (1, 3, 2))
    x_to = [xp * SIDE + z, xm * SIDE + z]
    z_to = [x * SIDE + zp, x * SIDE + zm]
    bits = []
    step = replicas // 2
    while step:
        bits.append(step)
        step //= 2
    halves = [lax.rem(lax.div(rep, b), 2) for b in bits]
    partners = [rep + b - 2 * b * h for b, h in zip(bits, halves)]

    barrier = pltpu.get_barrier_semaphore()
    for to in x_to + z_to:
        pl.semaphore_signal(barrier, inc=1, device_id={"fsdp": to}, device_id_type=MESH)
    for to in partners:
        pl.semaphore_signal(barrier, inc=1, device_id={"replica": to}, device_id_type=MESH)

    loads = [
        pltpu.make_async_copy(src, dst, in_sem.at[k])
        for k, (src, dst) in enumerate(
            [(w_hbm, w), (act_hbm, act), (tgt_hbm, tgt), (m1_hbm, m1), (m2_hbm, m2)]
        )
    ]
    for load in loads:
        load.start()

    top, low_half, high_half = pl.ds(0, ra), pl.ds(0, ha), pl.ds(ha, ha)
    end, low_end, high_end = pl.ds(ra, rb), pl.ds(ra, hb), pl.ds(ra + hb, hb)
    every = pl.ds(0, SIDE)
    sent = {}

    def send(c, phase, pairs, to):
        copies = []
        for d in range(2):
            src, dst = pairs[d]
            copies.append(
                pltpu.make_async_remote_copy(
                    src_ref=src,
                    dst_ref=dst,
                    send_sem=ssem.at[c, phase, d],
                    recv_sem=rsem.at[c, phase, d],
                    device_id={"fsdp": to[d]},
                    device_id_type=MESH,
                )
            )
        for copy in copies:
            copy.start()
        sent[c, phase] = copies

    def arrive(c, phase):
        for copy in sent[c, phase]:
            copy.wait_recv()

    def same(*refs):
        return [(r, r) for r in refs]

    def cols(c):
        return pl.ds(c * cw, cw)

    def a0(c):
        wf[c, x, z] = w[:, cols(c)].astype(BF16)
        own = wf.at[c, x, z, top]
        send(c, 0, same(own, own), z_to)
        own = wf.at[c, x, z, end]
        send(c, 1, same(own, own), x_to)

    def a1(c):
        arrive(c, 0)
        send(c, 2, same(wf.at[c, x, zm, low_half], wf.at[c, x, zp, high_half]), z_to)
        arrive(c, 1)
        send(c, 3, same(wf.at[c, xm, z, low_end], wf.at[c, xp, z, high_end]), x_to)

    def a2(c):
        arrive(c, 2)
        own = wf.at[c, x, every, top]
        send(c, 4, same(own, own), x_to)
        arrive(c, 3)
        own = wf.at[c, every, z, end]
        send(c, 5, same(own, own), z_to)

    def a3(c):
        arrive(c, 4)
        send(c, 6, same(wf.at[c, xm, every, low_half], wf.at[c, xp, every, high_half]), x_to)
        arrive(c, 5)
        send(c, 7, same(wf.at[c, every, zm, low_end], wf.at[c, every, zp, high_end]), z_to)

    def a4(c):
        arrive(c, 6)
        arrive(c, 7)

    def compute(c):
        total = None
        for g in range(SIDE):
            term = jnp.dot(
                act[:, pl.ds(g * group, group)],
                wf[c, g].reshape(group, cw),
                preferred_element_type=F32,
            )
            total = term if total is None else total + term
        values = total * scale
        err[...] = ((values - tgt[:, cols(c)].astype(F32)) / batch).astype(BF16)
        for g in (x2, xp, xm, x):
            part = jnp.dot(
                act_t[pl.ds(pl.multiple_of(g * group, group), group), :],
                err[...],
                preferred_element_type=F32,
            )
            pt[c, g] = part.astype(BF16).reshape(SIDE, rows, cw)
            if g is x2:
                send(
                    c,
                    8,
                    [
                        (pt.at[c, x2, every, low_half], rxh.at[c, 0]),
                        (pt.at[c, x2, every, high_half], rxh.at[c, 1]),
                    ],
                    x_to,
                )
        send(
            c,
            9,
            [
                (pt.at[c, every, z2, low_end], bzh.at[c, 0]),
                (pt.at[c, every, z2, high_end], bzh.at[c, 1]),
            ],
            z_to,
        )

    def add(c, i, j, part, *terms):
        total = pt[c, i, j, part, :].astype(F32)
        for term in terms:
            total = total + term.astype(F32)
        pt[c, i, j, part, :] = total.astype(BF16)

    def r1(c):
        arrive(c, 8)
        for k in range(SIDE):
            add(c, xp, k, low_half, rxh[c, 0, k])
            add(c, xm, k, high_half, rxh[c, 1, k])
        send(
            c,
            10,
            [
                (pt.at[c, xp, every, top], rxf.at[c, 0]),
                (pt.at[c, xm, every, top], rxf.at[c, 1]),
            ],
            x_to,
        )
        arrive(c, 9)
        for k in range(SIDE):
            add(c, k, zp, low_end, bzh[c, 0, k])
            add(c, k, zm, high_end, bzh[c, 1, k])
        send(
            c,
            11,
            [
                (pt.at[c, every, zp, end], bzf.at[c, 0]),
                (pt.at[c, every, zm, end], bzf.at[c, 1]),
            ],
            z_to,
        )

    def r2(c):
        arrive(c, 10)
        for k in range(SIDE):
            add(c, x, k, top, rxf[c, 0, k], rxf[c, 1, k])
        send(
            c,
            12,
            [
                (pt.at[c, x, z2, low_half], rzh.at[c, 0]),
                (pt.at[c, x, z2, high_half], rzh.at[c, 1]),
            ],
            z_to,
        )
        arrive(c, 11)
        for k in range(SIDE):
            add(c, k, z, end, bzf[c, 0, k], bzf[c, 1, k])
        send(
            c,
            13,
            [
                (pt.at[c, x2, z, low_end], bxh.at[c, 0]),
                (pt.at[c, x2, z, high_end], bxh.at[c, 1]),
            ],
            x_to,
        )

    def r3(c):
        arrive(c, 12)
        add(c, x, zp, low_half, rzh[c, 0])
        add(c, x, zm, high_half, rzh[c, 1])
        send(
            c,
            14,
            [(pt.at[c, x, zp, top], rzf.at[c, 0]), (pt.at[c, x, zm, top], rzf.at[c, 1])],
            z_to,
        )
        arrive(c, 13)
        add(c, xp, z, low_end, bxh[c, 0])
        add(c, xm, z, high_end, bxh[c, 1])
        send(
            c,
            15,
            [(pt.at[c, xp, z, end], bxf.at[c, 0]), (pt.at[c, xm, z, end], bxf.at[c, 1])],
            x_to,
        )

    frag = frag_ref[0]
    index = lax.bitwise_and(frag, FRAGS - 1)
    rate = 0.4 + 0.6 * frag.astype(F32) / WINDOWS
    width = cw * nc // FRAGS

    def r4(c):
        chosen = index == (c * cw) // width
        inside = pl.ds((c * cw) % width, cw)
        for phase, part, far in ((14, top, rzf), (15, end, bxf)):
            arrive(c, phase)
            grad = pt[c, x, z, part, :].astype(F32)
            grad = (grad + far[c, 0].astype(F32) + far[c, 1].astype(F32)) * scale
            old = w[part, cols(c)]
            moment1 = 0.9 * m1[part, cols(c)] + 0.1 * grad
            moment2 = 0.95 * m2[part, cols(c)] + 0.05 * grad * grad
            stepped = old - 0.25 * (moment1 / (jnp.sqrt(moment2) + 1e-08) + 0.1 * old)
            mixed = 0.5 * anc_full[part, inside] + 0.5 * stepped
            nw[part, cols(c)] = jnp.where(chosen, mixed, stepped)
        copy = pltpu.make_async_copy(nw.at[:, cols(c)], nw_hbm.at[:, cols(c)], out_sem.at[c])
        copy.start()
        sent["out", c] = copy

    spans = []
    base = 0
    share = width // replicas
    for b, h in zip(bits, halves):
        size = b * share
        spans.append((base, base + h * size, base + (1 - h) * size, size))
        base = base + h * size
    own_rows = pl.ds(pl.multiple_of(base, share), share)

    def trade(k, n, src, dst):
        copy = pltpu.make_async_remote_copy(
            src_ref=src,
            dst_ref=dst,
            send_sem=osend.at[n],
            recv_sem=orecv.at[n],
            device_id={"replica": partners[k]},
            device_id_type=MESH,
        )
        copy.start()
        sent["outer", n] = copy

    def halve(k):
        _, keep, give, size = spans[k]
        trade(
            k,
            k,
            old_t.at[pl.ds(pl.multiple_of(give, share), size)],
            got.at[pl.ds(size, size)],
        )

    def halve_done(k):
        _, keep, give, size = spans[k]
        sent["outer", k].wait_recv()
        kept = pl.ds(pl.multiple_of(keep, share), size)
        old_t[kept, :] = old_t[kept, :] + got[pl.ds(size, size), :]

    def double(k):
        _, keep, give, size = spans[k]
        part = anc_t.at[pl.ds(pl.multiple_of(keep, share), size)]
        trade(k, len(bits) + k, part, part)

    def outer_begin():
        picked = w[:, pl.ds(0, width)]
        for k in range(1, FRAGS):
            picked = jnp.where(index == k, w[:, pl.ds(k * width, width)], picked)
        tall[pl.ds(0, rows), :] = picked
        tall[pl.ds(rows, LANES - rows), :] = jnp.zeros((LANES - rows, width), F32)
        old_t[...] = tall[...].T
        halve(0)

    def outer_update():
        mean = old_t[own_rows, pl.ds(0, rows)] / replicas
        anchor, moment = anc_ref[0], mom_ref[0]
        for k in range(1, FRAGS):
            anchor = jnp.where(index == k, anc_ref[k], anchor)
            moment = jnp.where(index == k, mom_ref[k], moment)
        outer = anchor - mean
        moment = 0.9 * moment + outer
        anchor = anchor - rate * (outer + 0.9 * moment)
        for k in range(FRAGS):
            na_ref[k] = jnp.where(index == k, anchor, anc_ref[k])
            nm_ref[k] = jnp.where(index == k, moment, mom_ref[k])
        anc_t[own_rows, pl.ds(0, rows)] = anchor
        anc_t[own_rows, pl.ds(rows, LANES - rows)] = jnp.zeros((share, LANES - rows), F32)

    def outer_end():
        tall[...] = anc_t[...].T
        anc_full[...] = tall[pl.ds(0, rows), :]

    def turn(k, count):
        tiles = depth // 128 // count

        def one(i, carry):
            at = pl.ds(pl.multiple_of((k * tiles + i) * 128, 128), 128)
            act_t[at, :] = act[:, at].T
            return carry

        lax.fori_loop(0, tiles, one, 0)

    last = len(bits) - 1
    loads[0].wait()
    pl.semaphore_wait(barrier, 4 + len(bits))
    a0(0)
    outer_begin()
    a1(0)
    a0(1)
    loads[1].wait()
    turn(0, 4)
    a2(0)
    a1(1)
    turn(1, 4)
    a2(1)
    a0(2)
    turn(2, 4)
    a3(0)
    turn(3, 4)
    for load in loads[2:]:
        load.wait()
    extra = []
    for k in range(last):
        extra.append(lambda k=k: (halve_done(k), halve(k + 1)))
    extra.append(lambda: (halve_done(last), outer_update(), double(last)))
    for k in range(last - 1, -1, -1):
        extra.append(lambda k=k: (sent["outer", len(bits) + k + 1].wait_recv(), double(k)))
    extra.append(lambda: (sent["outer", len(bits)].wait_recv(), outer_end()))
    for i in range(nc):
        a4(i)
        compute(i)
        if i >= 2:
            r4(i - 2)
        if i + 1 < nc:
            a3(i + 1)
        for _ in range(2):
            if extra:
                extra.pop(0)()
        if i >= 1:
            r2(i - 1)
        if i + 2 < nc:
            a1(i + 2)
            a2(i + 2)
        if i + 3 < nc:
            a0(i + 3)
        while extra and i == 1:
            extra.pop(0)()
        r1(i)
        if i >= 1:
            r3(i - 1)
    r2(nc - 1)
    r4(nc - 2)
    r3(nc - 1)
    r4(nc - 1)
    for key, copies in sent.items():
        if key[0] == "out":
            copies.wait()
        elif key[0] == "outer":
            copies.wait_send()
        else:
            for copy in copies:
                copy.wait_send()


def shards(activations, teacher, weights, first_moment, second_moment, anchor, momentum, fragment):
    tokens, depth = activations.shape[1:]
    rows, width = weights.shape[1:]
    replicas = lax.axis_size("replica")
    share = anchor.shape[2]
    whole = share * replicas
    cw = width // CHUNKS
    ra, rb = ROWS_A, rows - ROWS_A
    batch = tokens * lax.axis_size("fsdp")
    bits = replicas.bit_length() - 1
    vmem = pltpu.VMEM
    anywhere = pl.BlockSpec(memory_space=pl.ANY)
    inside = pl.BlockSpec(memory_space=pltpu.VMEM)
    new_w, new_a, new_m = pl.pallas_call(
        functools.partial(kernel, batch),
        out_shape=(
            jax.ShapeDtypeStruct((rows, width), F32),
            jax.ShapeDtypeStruct((FRAGS, share, rows), F32),
            jax.ShapeDtypeStruct((FRAGS, share, rows), F32),
        ),
        in_specs=[pl.BlockSpec(memory_space=pltpu.SMEM)] + [anywhere] * 5 + [inside] * 2,
        out_specs=(anywhere, inside, inside),
        scratch_shapes=[
            vmem((tokens, depth), BF16),
            vmem((depth, tokens), BF16),
            vmem((tokens, width), BF16),
            vmem((rows, width), F32),
            vmem((rows, width), F32),
            vmem((rows, width), F32),
            vmem((rows, width), F32),
            vmem((CHUNKS, SIDE, SIDE, rows, cw), BF16),
            vmem((CHUNKS, SIDE, SIDE, rows, cw), BF16),
            vmem((tokens, cw), BF16),
            vmem((8, 128), F32),
            vmem((CHUNKS, 2, SIDE, ra // 2, cw), BF16),
            vmem((CHUNKS, 2, SIDE, ra, cw), BF16),
            vmem((CHUNKS, 2, ra // 2, cw), BF16),
            vmem((CHUNKS, 2, ra, cw), BF16),
            vmem((CHUNKS, 2, SIDE, rb // 2, cw), BF16),
            vmem((CHUNKS, 2, SIDE, rb, cw), BF16),
            vmem((CHUNKS, 2, rb // 2, cw), BF16),
            vmem((CHUNKS, 2, rb, cw), BF16),
            vmem((LANES, whole), F32),
            vmem((whole, LANES), F32),
            vmem((whole, LANES), F32),
            vmem((rows, whole), F32),
            vmem((whole, LANES), F32),
            pltpu.SemaphoreType.DMA((5,)),
            pltpu.SemaphoreType.DMA((CHUNKS,)),
            pltpu.SemaphoreType.DMA((CHUNKS, 16, 2)),
            pltpu.SemaphoreType.DMA((CHUNKS, 16, 2)),
            pltpu.SemaphoreType.DMA((2 * bits,)),
            pltpu.SemaphoreType.DMA((2 * bits,)),
        ],
        compiler_params=pltpu.CompilerParams(
            collective_id=0, has_side_effects=True, vmem_limit_bytes=60 * 2**20
        ),
    )(
        fragment,
        activations[0],
        teacher[0],
        weights[0],
        first_moment[0],
        second_moment[0],
        jnp.swapaxes(anchor, 1, 2),
        jnp.swapaxes(momentum, 1, 2),
    )
    return (new_w[None], jnp.swapaxes(new_a, 1, 2), jnp.swapaxes(new_m, 1, 2))


def solution(mesh):
    in_specs = (
        P("replica", "fsdp", None),
        P("replica", "fsdp", None),
        P("replica", "fsdp", None),
        P("replica", "fsdp", None),
        P("replica", "fsdp", None),
        P(None, "fsdp", "replica"),
        P(None, "fsdp", "replica"),
        P(),
    )
    out_specs = (P("replica", "fsdp", None), P(None, "fsdp", "replica"), P(None, "fsdp", "replica"))
    return jax.shard_map(shards, mesh=mesh, in_specs=in_specs, out_specs=out_specs, check_vma=False)
```

```python
import functools
import math

import jax
import jax.numpy as jnp
from jax import lax
from jax.experimental import pallas as pl
from jax.experimental.pallas import tpu as pltpu
from jax.sharding import PartitionSpec as P

FRAGS = 4
WINDOWS = 256
SIDE = 4
CHUNKS = 4
ROWS_A = 224
LANES = 384
PHASES = 32
SPLIT_GATHER = (0, 1)
SPLIT_SCATTER = (2, 3)
ORDER = (
    ("a0", 1), ("a1x", 1), ("o", 0), ("a0", 0), ("a0", 2), ("o", 0), ("a1z", 1), ("o", 0), ("a3x0", 0),
    ("a1x", 2), ("a1x", 0), ("T", 0), ("a1z", 0), ("a2z", 0), ("a2x", 1), ("o", 0), ("a2x", 0), ("T", 0),
    ("T", 0), ("a3x1", 0), ("a1z", 2), ("a3x2", 1), ("a3z", 0), ("o", 0), ("a0", 3), ("a3x1", 1), ("o", 0),
    ("a3x2", 0), ("a2x", 2), ("a4", 0), ("a3x0", 1), ("a2z", 1), ("T", 0), ("a2z", 2), ("C", 0), ("a3z", 1),
    ("a3x", 2), ("r1x", 0), ("r1z", 0), ("o", 0), ("o", 0), ("a1z", 3), ("a1x", 3), ("a4", 1), ("a3z", 2),
    ("C", 1), ("a2x", 3), ("a2z", 3), ("r1z", 1), ("a4", 2), ("r1x", 1), ("C", 2), ("a3z", 3), ("r1z", 2),
    ("a3x", 3), ("r2z", 0), ("r2z", 1), ("r2x", 0), ("r1x0", 2), ("r1x1", 2), ("r3z", 1), ("r3z", 0),
    ("a4", 3), ("C", 3), ("r2x", 1), ("r2z1", 2), ("o", 0), ("r1x0", 3), ("r2x", 2), ("r2z0", 2), ("r1z", 3),
    ("r1x1", 3), ("r3x", 0), ("r2z0", 3), ("r2z1", 3), ("r3z", 2), ("r4", 0), ("r1x2", 3), ("r2x", 3),
    ("r1x2", 2), ("r3z", 3), ("r3x", 1), ("r3x", 3), ("r3x", 2), ("r2z2", 2), ("r4", 1), ("r4", 2),
    ("r2z2", 3), ("r4", 3),
)
MESH = pl.DeviceIdType.MESH
F32 = jnp.float32
BF16 = jnp.bfloat16


def exchange_bits(replicas):
    bits = [1 << k for k in range(replicas.bit_length() - 1)]
    return bits[:1] + bits[2:] + bits[1:2]


def place(replica, replicas):
    at, size = 0, replicas // 2
    for bit in exchange_bits(replicas):
        at += size if replica & bit else 0
        size //= 2
    return at


def kernel(
    batch,
    frag_ref,
    act_hbm,
    tgt_hbm,
    w_hbm,
    m1_hbm,
    m2_hbm,
    anc_ref,
    mom_ref,
    nw_hbm,
    na_ref,
    nm_ref,
    act,
    act_t,
    tgt,
    w,
    m1,
    m2,
    nw,
    wf,
    pt,
    err,
    rxh,
    rxf,
    rzh,
    rzf,
    bzh,
    bzf,
    bxh,
    bxf,
    tall,
    old_t,
    anc_t,
    anc_full,
    got,
    in_sem,
    out_sem,
    ssem,
    rsem,
    osend,
    orecv,
):
    nc, rows, cw = wf.shape[0], wf.shape[3], wf.shape[4]
    ra, rb = ROWS_A, rows - ROWS_A
    ha, hb = ra // 2, rb // 2
    depth = act.shape[1]
    scale = 1.0 / math.sqrt(depth)
    group = SIDE * rows

    me = lax.axis_index("fsdp")
    rep = lax.axis_index("replica")
    replicas = lax.axis_size("replica")
    x, z = lax.div(me, SIDE), lax.rem(me, SIDE)
    xp, xm, x2 = (lax.rem(x + k, SIDE) for k in (1, 3, 2))
    zp, zm, z2 = (lax.rem(z + k, SIDE) for k in (1, 3, 2))
    x_to = [xp * SIDE + z, xm * SIDE + z]
    z_to = [x * SIDE + zp, x * SIDE + zm]
    bits = exchange_bits(replicas)
    halves = [lax.rem(lax.div(rep, b), 2) for b in bits]
    partners = [rep + b - 2 * b * h for b, h in zip(bits, halves)]

    barrier = pltpu.get_barrier_semaphore()
    for to in x_to + z_to:
        pl.semaphore_signal(barrier, inc=1, device_id={"fsdp": to}, device_id_type=MESH)
    for to in partners:
        pl.semaphore_signal(barrier, inc=1, device_id={"replica": to}, device_id_type=MESH)

    loads = [
        pltpu.make_async_copy(src, dst, in_sem.at[k])
        for k, (src, dst) in enumerate(
            [(w_hbm, w), (act_hbm, act), (tgt_hbm, tgt), (m1_hbm, m1), (m2_hbm, m2)]
        )
    ]
    for load in loads:
        load.start()

    top, low_half, high_half = pl.ds(0, ra), pl.ds(0, ha), pl.ds(ha, ha)
    end, low_end, high_end = pl.ds(ra, rb), pl.ds(ra, hb), pl.ds(ra + hb, hb)
    every = pl.ds(0, SIDE)
    sent = {}

    def send(c, phase, pairs, to):
        copies = []
        for d in range(2):
            src, dst = pairs[d]
            copies.append(
                pltpu.make_async_remote_copy(
                    src_ref=src,
                    dst_ref=dst,
                    send_sem=ssem.at[c, phase, d],
                    recv_sem=rsem.at[c, phase, d],
                    device_id={"fsdp": to[d]},
                    device_id_type=MESH,
                )
            )
        for copy in copies:
            copy.start()
        sent[c, phase] = copies

    def arrive(c, phase):
        for copy in sent[c, phase]:
            copy.wait_recv()

    def same(*refs):
        return [(r, r) for r in refs]

    def cols(c):
        return pl.ds(c * cw, cw)

    def a0(c):
        wf[c, x, z] = w[:, cols(c)].astype(BF16)
        own = wf.at[c, x, z, top]
        send(c, 0, same(own, own), z_to)
        if c in SPLIT_GATHER:
            send(c, 4, same(own, own), x_to)
        own = wf.at[c, x, z, end]
        send(c, 1, same(own, own), x_to)

    def a1z(c):
        arrive(c, 0)
        send(c, 2, same(wf.at[c, x, zm, low_half], wf.at[c, x, zp, high_half]), z_to)
        if c in SPLIT_GATHER:
            for phase, k in ((16, zm), (17, zp)):
                far = wf.at[c, x, k, top]
                send(c, phase, same(far, far), x_to)

    def a1x(c):
        arrive(c, 1)
        send(c, 3, same(wf.at[c, xm, z, low_end], wf.at[c, xp, z, high_end]), x_to)

    def a2x(c):
        arrive(c, 2)
        far = wf.at[c, x, z2, top] if c in SPLIT_GATHER else wf.at[c, x, every, top]
        send(c, 18 if c in SPLIT_GATHER else 4, same(far, far), x_to)

    def a2z(c):
        arrive(c, 3)
        own = wf.at[c, every, z, end]
        send(c, 5, same(own, own), z_to)

    def pass_on(c, phase, then, k):
        arrive(c, phase)
        send(c, then, same(wf.at[c, xm, k, low_half], wf.at[c, xp, k, high_half]), x_to)

    def a3x(c):
        pass_on(c, 4, 6, every)

    def a3x0(c):
        pass_on(c, 4, 6, z)

    def a3x1(c):
        pass_on(c, 16, 19, zm)
        pass_on(c, 17, 20, zp)

    def a3x2(c):
        pass_on(c, 18, 21, z2)

    def a3z(c):
        arrive(c, 5)
        send(c, 7, same(wf.at[c, every, zm, low_end], wf.at[c, every, zp, high_end]), z_to)

    def a4(c):
        for phase in (6, 19, 20, 21, 7) if c in SPLIT_GATHER else (6, 7):
            arrive(c, phase)

    def compute(c):
        total = None
        for g in range(SIDE):
            term = jnp.dot(
                act[:, pl.ds(g * group, group)],
                wf[c, g].reshape(group, cw),
                preferred_element_type=F32,
            )
            total = term if total is None else total + term
        values = total * scale
        err[...] = ((values - tgt[:, cols(c)].astype(F32)) / batch).astype(BF16)
        for g in (x2, xp, xm, x):
            part = jnp.dot(
                act_t[pl.ds(pl.multiple_of(g * group, group), group), :],
                err[...],
                preferred_element_type=F32,
            )
            pt[c, g] = part.astype(BF16).reshape(SIDE, rows, cw)
            if g is x2:
                for phase, k in by_shard(c, 8):
                    low = (pt.at[c, x2, k, low_half], rxh.at[c, 0, k])
                    high = (pt.at[c, x2, k, high_half], rxh.at[c, 1, k])
                    send(c, phase, [low, high], x_to)
        send(
            c,
            9,
            [
                (pt.at[c, every, z2, low_end], bzh.at[c, 0]),
                (pt.at[c, every, z2, high_end], bzh.at[c, 1]),
            ],
            z_to,
        )

    def by_shard(c, first):
        if c not in SPLIT_SCATTER:
            return [(first, every)]
        base = 22 if first == 8 else 25
        return [(first, z2), (base, zm), (base + 1, zp), (base + 2, z)]

    def add(c, i, j, part, *terms):
        total = pt[c, i, j, part, :].astype(F32)
        for term in terms:
            total = total + term.astype(F32)
        pt[c, i, j, part, :] = total.astype(BF16)

    def first_sum(c, groups):
        for (phase, k), (then, _) in groups:
            arrive(c, phase)
            for j in range(SIDE) if k is every else (k,):
                add(c, xp, j, low_half, rxh[c, 0, j])
                add(c, xm, j, high_half, rxh[c, 1, j])
            right = (pt.at[c, xp, k, top], rxf.at[c, 0, k])
            left = (pt.at[c, xm, k, top], rxf.at[c, 1, k])
            send(c, then, [right, left], x_to)

    def groups_of(c):
        return list(zip(by_shard(c, 8), by_shard(c, 10)))

    def r1x(c):
        first_sum(c, groups_of(c))

    def r1x0(c):
        first_sum(c, groups_of(c)[:1])

    def r1x1(c):
        first_sum(c, groups_of(c)[1:3])

    def r1x2(c):
        first_sum(c, groups_of(c)[3:])

    def r1z(c):
        arrive(c, 9)
        for k in range(SIDE):
            add(c, k, zp, low_end, bzh[c, 0, k])
            add(c, k, zm, high_end, bzh[c, 1, k])
        send(
            c,
            11,
            [
                (pt.at[c, every, zp, end], bzf.at[c, 0]),
                (pt.at[c, every, zm, end], bzf.at[c, 1]),
            ],
            z_to,
        )

    def second_sum(c, groups):
        for phase, k in groups:
            arrive(c, phase)
            for j in range(SIDE) if k is every else (k,):
                add(c, x, j, top, rxf[c, 0, j], rxf[c, 1, j])

    def send_far(c):
        low = (pt.at[c, x, z2, low_half], rzh.at[c, 0])
        high = (pt.at[c, x, z2, high_half], rzh.at[c, 1])
        send(c, 12, [low, high], z_to)

    def r2z(c):
        second_sum(c, by_shard(c, 10))
        send_far(c)

    def r2z0(c):
        second_sum(c, by_shard(c, 10)[:1])
        send_far(c)

    def r2z1(c):
        second_sum(c, by_shard(c, 10)[1:3])

    def r2z2(c):
        second_sum(c, by_shard(c, 10)[3:])

    def r2x(c):
        arrive(c, 11)
        for k in range(SIDE):
            add(c, k, z, end, bzf[c, 0, k], bzf[c, 1, k])
        send(
            c,
            13,
            [
                (pt.at[c, x2, z, low_end], bxh.at[c, 0]),
                (pt.at[c, x2, z, high_end], bxh.at[c, 1]),
            ],
            x_to,
        )

    def r3z(c):
        arrive(c, 12)
        add(c, x, zp, low_half, rzh[c, 0])
        add(c, x, zm, high_half, rzh[c, 1])
        send(
            c,
            14,
            [(pt.at[c, x, zp, top], rzf.at[c, 0]), (pt.at[c, x, zm, top], rzf.at[c, 1])],
            z_to,
        )

    def r3x(c):
        arrive(c, 13)
        add(c, xp, z, low_end, bxh[c, 0])
        add(c, xm, z, high_end, bxh[c, 1])
        send(
            c,
            15,
            [(pt.at[c, xp, z, end], bxf.at[c, 0]), (pt.at[c, xm, z, end], bxf.at[c, 1])],
            x_to,
        )

    frag = frag_ref[0]
    index = lax.bitwise_and(frag, FRAGS - 1)
    rate = 0.4 + 0.6 * frag.astype(F32) / WINDOWS
    width = cw * nc // FRAGS

    def r4(c):
        chosen = index == (c * cw) // width
        inside = pl.ds((c * cw) % width, cw)
        for phase, part, far in ((14, top, rzf), (15, end, bxf)):
            arrive(c, phase)
            grad = pt[c, x, z, part, :].astype(F32)
            grad = (grad + far[c, 0].astype(F32) + far[c, 1].astype(F32)) * scale
            old = w[part, cols(c)]
            moment1 = 0.9 * m1[part, cols(c)] + 0.1 * grad
            moment2 = 0.95 * m2[part, cols(c)] + 0.05 * grad * grad
            stepped = old - 0.25 * (moment1 / (jnp.sqrt(moment2) + 1e-08) + 0.1 * old)
            mixed = 0.5 * anc_full[part, inside] + 0.5 * stepped
            nw[part, cols(c)] = jnp.where(chosen, mixed, stepped)
        copy = pltpu.make_async_copy(nw.at[:, cols(c)], nw_hbm.at[:, cols(c)], out_sem.at[c])
        copy.start()
        sent["out", c] = copy

    spans = []
    base = 0
    share = width // replicas
    for k, h in enumerate(halves):
        size = width >> (k + 1)
        spans.append((base, base + h * size, base + (1 - h) * size, size))
        base = base + h * size
    own_rows = pl.ds(pl.multiple_of(base, share), share)

    def trade(k, n, src, dst):
        copy = pltpu.make_async_remote_copy(
            src_ref=src,
            dst_ref=dst,
            send_sem=osend.at[n],
            recv_sem=orecv.at[n],
            device_id={"replica": partners[k]},
            device_id_type=MESH,
        )
        copy.start()
        sent["outer", n] = copy

    def halve(k):
        _, keep, give, size = spans[k]
        trade(
            k,
            k,
            old_t.at[pl.ds(pl.multiple_of(give, share), size)],
            got.at[pl.ds(size, size)],
        )

    def halve_done(k):
        _, keep, give, size = spans[k]
        sent["outer", k].wait_recv()
        kept = pl.ds(pl.multiple_of(keep, share), size)
        old_t[kept, :] = old_t[kept, :] + got[pl.ds(size, size), :]

    def double(k):
        _, keep, give, size = spans[k]
        part = anc_t.at[pl.ds(pl.multiple_of(keep, share), size)]
        trade(k, len(bits) + k, part, part)

    def outer_begin():
        picked = w[:, pl.ds(0, width)]
        for k in range(1, FRAGS):
            picked = jnp.where(index == k, w[:, pl.ds(k * width, width)], picked)
        tall[pl.ds(0, rows), :] = picked
        tall[pl.ds(rows, LANES - rows), :] = jnp.zeros((LANES - rows, width), F32)
        anc_t[...] = tall[...].T
        for r in range(replicas):
            at = pl.ds(place(r, replicas) * share, share)
            old_t[at, :] = anc_t[pl.ds(r * share, share), :]
        halve(0)

    def outer_update():
        mean = old_t[own_rows, pl.ds(0, rows)] / replicas
        anchor, moment = anc_ref[0], mom_ref[0]
        for k in range(1, FRAGS):
            anchor = jnp.where(index == k, anc_ref[k], anchor)
            moment = jnp.where(index == k, mom_ref[k], moment)
        outer = anchor - mean
        moment = 0.9 * moment + outer
        anchor = anchor - rate * (outer + 0.9 * moment)
        for k in range(FRAGS):
            na_ref[k] = jnp.where(index == k, anchor, anc_ref[k])
            nm_ref[k] = jnp.where(index == k, moment, mom_ref[k])
        anc_t[own_rows, pl.ds(0, rows)] = anchor
        anc_t[own_rows, pl.ds(rows, LANES - rows)] = jnp.zeros((share, LANES - rows), F32)

    def outer_end():
        for r in range(replicas):
            at = pl.ds(place(r, replicas) * share, share)
            got[pl.ds(r * share, share), :] = anc_t[at, :]
        tall[...] = got[...].T
        anc_full[...] = tall[pl.ds(0, rows), :]

    def turn(k, count):
        tiles = depth // 128 // count

        def one(i, carry):
            at = pl.ds(pl.multiple_of((k * tiles + i) * 128, 128), 128)
            act_t[at, :] = act[:, at].T
            return carry

        lax.fori_loop(0, tiles, one, 0)

    steps = len(bits)
    outer = [outer_begin]
    for k in range(1, steps):
        outer.append(lambda k=k: (halve_done(k - 1), halve(k)))
    outer.append(lambda: (halve_done(steps - 1), outer_update(), double(steps - 1)))
    for k in range(steps - 1, 0, -1):
        outer.append(lambda k=k: (sent["outer", steps + k].wait_recv(), double(k - 1)))
    outer.append(lambda: (sent["outer", steps].wait_recv(), outer_end()))

    events = {
        "a0": a0,
        "a1z": a1z,
        "a1x": a1x,
        "a2x": a2x,
        "a2z": a2z,
        "a3x": a3x,
        "a3x0": a3x0,
        "a3x1": a3x1,
        "a3x2": a3x2,
        "a3z": a3z,
        "a4": a4,
        "C": compute,
        "r1x": r1x,
        "r1x0": r1x0,
        "r1x1": r1x1,
        "r1x2": r1x2,
        "r1z": r1z,
        "r2z": r2z,
        "r2z0": r2z0,
        "r2z1": r2z1,
        "r2z2": r2z2,
        "r2x": r2x,
        "r3z": r3z,
        "r3x": r3x,
        "r4": r4,
        "T": lambda c: turns.pop(0)(),
        "o": lambda c: outer.pop(0)(),
    }
    turns = [lambda: (loads[1].wait(), turn(0, 4)), lambda: turn(1, 4), lambda: turn(2, 4)]
    turns.append(lambda: (turn(3, 4), [load.wait() for load in loads[2:]]))
    loads[0].wait()
    pl.semaphore_wait(barrier, 4 + len(bits))
    for event, c in ORDER:
        events[event](c)
    for key, copies in sent.items():
        if key[0] == "out":
            copies.wait()
        elif key[0] == "outer":
            copies.wait_send()
        else:
            for copy in copies:
                copy.wait_send()


def shards(activations, teacher, weights, first_moment, second_moment, anchor, momentum, fragment):
    tokens, depth = activations.shape[1:]
    rows, width = weights.shape[1:]
    replicas = lax.axis_size("replica")
    share = anchor.shape[2]
    whole = share * replicas
    cw = width // CHUNKS
    ra, rb = ROWS_A, rows - ROWS_A
    batch = tokens * lax.axis_size("fsdp")
    bits = replicas.bit_length() - 1
    vmem = pltpu.VMEM
    anywhere = pl.BlockSpec(memory_space=pl.ANY)
    inside = pl.BlockSpec(memory_space=pltpu.VMEM)
    new_w, new_a, new_m = pl.pallas_call(
        functools.partial(kernel, batch),
        out_shape=(
            jax.ShapeDtypeStruct((rows, width), F32),
            jax.ShapeDtypeStruct((FRAGS, share, rows), F32),
            jax.ShapeDtypeStruct((FRAGS, share, rows), F32),
        ),
        in_specs=[pl.BlockSpec(memory_space=pltpu.SMEM)] + [anywhere] * 5 + [inside] * 2,
        out_specs=(anywhere, inside, inside),
        scratch_shapes=[
            vmem((tokens, depth), BF16),
            vmem((depth, tokens), BF16),
            vmem((tokens, width), BF16),
            vmem((rows, width), F32),
            vmem((rows, width), F32),
            vmem((rows, width), F32),
            vmem((rows, width), F32),
            vmem((CHUNKS, SIDE, SIDE, rows, cw), BF16),
            vmem((CHUNKS, SIDE, SIDE, rows, cw), BF16),
            vmem((tokens, cw), BF16),
            vmem((CHUNKS, 2, SIDE, ra // 2, cw), BF16),
            vmem((CHUNKS, 2, SIDE, ra, cw), BF16),
            vmem((CHUNKS, 2, ra // 2, cw), BF16),
            vmem((CHUNKS, 2, ra, cw), BF16),
            vmem((CHUNKS, 2, SIDE, rb // 2, cw), BF16),
            vmem((CHUNKS, 2, SIDE, rb, cw), BF16),
            vmem((CHUNKS, 2, rb // 2, cw), BF16),
            vmem((CHUNKS, 2, rb, cw), BF16),
            vmem((LANES, whole), F32),
            vmem((whole, LANES), F32),
            vmem((whole, LANES), F32),
            vmem((rows, whole), F32),
            vmem((whole, LANES), F32),
            pltpu.SemaphoreType.DMA((5,)),
            pltpu.SemaphoreType.DMA((CHUNKS,)),
            pltpu.SemaphoreType.DMA((CHUNKS, PHASES, 2)),
            pltpu.SemaphoreType.DMA((CHUNKS, PHASES, 2)),
            pltpu.SemaphoreType.DMA((2 * bits,)),
            pltpu.SemaphoreType.DMA((2 * bits,)),
        ],
        compiler_params=pltpu.CompilerParams(
            collective_id=0, has_side_effects=True, vmem_limit_bytes=60 * 2**20
        ),
    )(
        fragment,
        activations[0],
        teacher[0],
        weights[0],
        first_moment[0],
        second_moment[0],
        jnp.swapaxes(anchor, 1, 2),
        jnp.swapaxes(momentum, 1, 2),
    )
    return (new_w[None], jnp.swapaxes(new_a, 1, 2), jnp.swapaxes(new_m, 1, 2))


def solution(mesh):
    in_specs = (
        P("replica", "fsdp", None),
        P("replica", "fsdp", None),
        P("replica", "fsdp", None),
        P("replica", "fsdp", None),
        P("replica", "fsdp", None),
        P(None, "fsdp", "replica"),
        P(None, "fsdp", "replica"),
        P(),
    )
    out_specs = (P("replica", "fsdp", None), P(None, "fsdp", "replica"), P(None, "fsdp", "replica"))
    return jax.shard_map(shards, mesh=mesh, in_specs=in_specs, out_specs=out_specs, check_vma=False)
```

```python
import functools
import math

import jax
import jax.numpy as jnp
from jax import lax
from jax.experimental import pallas as pl
from jax.experimental.pallas import tpu as pltpu
from jax.sharding import PartitionSpec as P

FRAGS = 4
WINDOWS = 256
SIDE = 4
CHUNKS = 4
ROWS_A = 224
LANES = 384
PHASES = 32
SPLIT_GATHER = (0, 1, 2)
SPLIT_SCATTER = (1, 2, 3)
ORDER = (
    ("a0", 0), ("a0", 2), ("a0", 1), ("a1x", 0), ("a1z", 0), ("a1x", 2), ("a1z", 2), ("a1z", 1), ("a1x", 1),
    ("a0", 3), ("T", 0), ("T", 0), ("a3x1", 0), ("a2x", 1), ("T", 0), ("a2x", 0), ("a2x", 2), ("a3x0", 0),
    ("a2z", 0), ("o", 0), ("a1z", 3), ("a3x0", 1), ("a2z", 1), ("a3x1", 1), ("a3x2", 0), ("a1x", 3),
    ("a3z", 0), ("a3z", 1), ("o", 0), ("a3x2", 2), ("a3x2", 1), ("a3x1", 2), ("T", 0), ("a2z", 2), ("o", 0),
    ("a3x0", 2), ("a2x", 3), ("a2z", 3), ("a4", 1), ("a4", 0), ("C", 0), ("a3z", 2), ("o", 0), ("C", 1),
    ("r1z", 0), ("r1x0", 1), ("a3x", 3), ("a4", 2), ("a3z", 3), ("C", 2), ("o", 0), ("r1x1", 1), ("r2z0", 1),
    ("r1z", 1), ("a4", 3), ("C", 3), ("r1x", 0), ("r1z", 2), ("r1x0", 2), ("r2z1", 1), ("r1x0", 3),
    ("r2x", 1), ("o", 0), ("r1x1", 3), ("r1z", 3), ("r3z", 1), ("o", 0), ("r2z0", 2), ("o", 0), ("r1x1", 2),
    ("r2z0", 3), ("r1x2", 1), ("r2x", 0), ("r2z", 0), ("r2z1", 3), ("r3z", 3), ("r2x", 2), ("r3z", 0),
    ("r2z1", 2), ("r1x2", 3), ("r3x", 0), ("r3z", 2), ("r2x", 3), ("r3x", 1), ("r2z2", 1), ("r1x2", 2),
    ("r3x", 3), ("r3x", 2), ("o", 0), ("r4", 0), ("r2z2", 3), ("r4", 1), ("r2z2", 2), ("r4", 3), ("r4", 2),
)
MESH = pl.DeviceIdType.MESH
F32 = jnp.float32
BF16 = jnp.bfloat16


def exchange_bits(replicas):
    bits = [1 << k for k in range(replicas.bit_length() - 1)]
    return bits[:1] + bits[2:] + bits[1:2]


def place(replica, replicas):
    at, size = 0, replicas // 2
    for bit in exchange_bits(replicas):
        at += size if replica & bit else 0
        size //= 2
    return at


def kernel(
    batch,
    frag_ref,
    act_hbm,
    tgt_hbm,
    w_hbm,
    m1_hbm,
    m2_hbm,
    anc_hbm,
    mom_hbm,
    nw_hbm,
    na_ref,
    nm_ref,
    act,
    act_t,
    tgt,
    w,
    m1,
    m2,
    nw,
    wf,
    pt,
    err,
    rxh,
    rxf,
    rzh,
    rzf,
    bzh,
    bzf,
    bxh,
    bxf,
    anc_ref,
    mom_ref,
    tall,
    old_t,
    anc_t,
    anc_full,
    got,
    in_sem,
    out_sem,
    ssem,
    rsem,
    osend,
    orecv,
):
    nc, rows, cw = wf.shape[0], wf.shape[3], wf.shape[4]
    ra, rb = ROWS_A, rows - ROWS_A
    ha, hb = ra // 2, rb // 2
    depth = act.shape[1]
    scale = 1.0 / math.sqrt(depth)
    group = SIDE * rows

    me = lax.axis_index("fsdp")
    rep = lax.axis_index("replica")
    replicas = lax.axis_size("replica")
    x, z = lax.div(me, SIDE), lax.rem(me, SIDE)
    xp, xm, x2 = (lax.rem(x + k, SIDE) for k in (1, 3, 2))
    zp, zm, z2 = (lax.rem(z + k, SIDE) for k in (1, 3, 2))
    x_to = [xp * SIDE + z, xm * SIDE + z]
    z_to = [x * SIDE + zp, x * SIDE + zm]
    bits = exchange_bits(replicas)
    halves = [lax.rem(lax.div(rep, b), 2) for b in bits]
    partners = [rep + b - 2 * b * h for b, h in zip(bits, halves)]

    barrier = pltpu.get_barrier_semaphore()
    for to in x_to + z_to:
        pl.semaphore_signal(barrier, inc=1, device_id={"fsdp": to}, device_id_type=MESH)
    for to in partners:
        pl.semaphore_signal(barrier, inc=1, device_id={"replica": to}, device_id_type=MESH)

    loads = [
        pltpu.make_async_copy(src, dst, in_sem.at[k])
        for k, (src, dst) in enumerate(
            [
                (w_hbm, w),
                (act_hbm, act),
                (tgt_hbm, tgt),
                (m1_hbm, m1),
                (m2_hbm, m2),
                (anc_hbm, anc_ref),
                (mom_hbm, mom_ref),
            ]
        )
    ]
    for load in loads:
        load.start()

    top, low_half, high_half = pl.ds(0, ra), pl.ds(0, ha), pl.ds(ha, ha)
    end, low_end, high_end = pl.ds(ra, rb), pl.ds(ra, hb), pl.ds(ra + hb, hb)
    every = pl.ds(0, SIDE)
    sent = {}

    def send(c, phase, pairs, to):
        copies = []
        for d in range(2):
            src, dst = pairs[d]
            copies.append(
                pltpu.make_async_remote_copy(
                    src_ref=src,
                    dst_ref=dst,
                    send_sem=ssem.at[c, phase, d],
                    recv_sem=rsem.at[c, phase, d],
                    device_id={"fsdp": to[d]},
                    device_id_type=MESH,
                )
            )
        for copy in copies:
            copy.start()
        sent[c, phase] = copies

    def arrive(c, phase):
        for copy in sent[c, phase]:
            copy.wait_recv()

    def same(*refs):
        return [(r, r) for r in refs]

    def cols(c):
        return pl.ds(c * cw, cw)

    def a0(c):
        wf[c, x, z] = w[:, cols(c)].astype(BF16)
        own = wf.at[c, x, z, top]
        send(c, 0, same(own, own), z_to)
        short = wf.at[c, x, z, end]
        send(c, 1, same(short, short), x_to)
        if c in SPLIT_GATHER:
            send(c, 4, same(own, own), x_to)

    def a1z(c):
        arrive(c, 0)
        send(c, 2, same(wf.at[c, x, zm, low_half], wf.at[c, x, zp, high_half]), z_to)
        if c in SPLIT_GATHER:
            for phase, k in ((16, zm), (17, zp)):
                far = wf.at[c, x, k, top]
                send(c, phase, same(far, far), x_to)

    def a1x(c):
        arrive(c, 1)
        send(c, 3, same(wf.at[c, xm, z, low_end], wf.at[c, xp, z, high_end]), x_to)

    def a2x(c):
        arrive(c, 2)
        far = wf.at[c, x, z2, top] if c in SPLIT_GATHER else wf.at[c, x, every, top]
        send(c, 18 if c in SPLIT_GATHER else 4, same(far, far), x_to)

    def a2z(c):
        arrive(c, 3)
        own = wf.at[c, every, z, end]
        send(c, 5, same(own, own), z_to)

    def pass_on(c, phase, then, k):
        arrive(c, phase)
        send(c, then, same(wf.at[c, xm, k, low_half], wf.at[c, xp, k, high_half]), x_to)

    def a3x(c):
        pass_on(c, 4, 6, every)

    def a3x0(c):
        pass_on(c, 4, 6, z)

    def a3x1(c):
        pass_on(c, 16, 19, zm)
        pass_on(c, 17, 20, zp)

    def a3x2(c):
        pass_on(c, 18, 21, z2)

    def a3z(c):
        arrive(c, 5)
        send(c, 7, same(wf.at[c, every, zm, low_end], wf.at[c, every, zp, high_end]), z_to)

    def a4(c):
        for phase in (6, 19, 20, 21, 7) if c in SPLIT_GATHER else (6, 7):
            arrive(c, phase)

    def compute(c):
        total = None
        for g in range(SIDE):
            term = jnp.dot(
                act[:, pl.ds(g * group, group)],
                wf[c, g].reshape(group, cw),
                preferred_element_type=F32,
            )
            total = term if total is None else total + term
        values = total * scale
        err[...] = ((values - tgt[:, cols(c)].astype(F32)) / batch).astype(BF16)
        for g in (x2, xp, xm, x):
            part = jnp.dot(
                act_t[pl.ds(pl.multiple_of(g * group, group), group), :],
                err[...],
                preferred_element_type=F32,
            )
            pt[c, g] = part.astype(BF16).reshape(SIDE, rows, cw)
            if g is x2:
                for phase, k in by_shard(c, 8):
                    low = (pt.at[c, x2, k, low_half], rxh.at[c, 0, k])
                    high = (pt.at[c, x2, k, high_half], rxh.at[c, 1, k])
                    send(c, phase, [low, high], x_to)
        send(
            c,
            9,
            [
                (pt.at[c, every, z2, low_end], bzh.at[c, 0]),
                (pt.at[c, every, z2, high_end], bzh.at[c, 1]),
            ],
            z_to,
        )

    def by_shard(c, first):
        if c not in SPLIT_SCATTER:
            return [(first, every)]
        base = 22 if first == 8 else 25
        return [(first, z2), (base, zm), (base + 1, zp), (base + 2, z)]

    def add(c, i, j, part, *terms):
        total = pt[c, i, j, part, :].astype(F32)
        for term in terms:
            total = total + term.astype(F32)
        pt[c, i, j, part, :] = total.astype(BF16)

    def first_sum(c, groups):
        for (phase, k), (then, _) in groups:
            arrive(c, phase)
            for j in range(SIDE) if k is every else (k,):
                add(c, xp, j, low_half, rxh[c, 0, j])
                add(c, xm, j, high_half, rxh[c, 1, j])
            right = (pt.at[c, xp, k, top], rxf.at[c, 0, k])
            left = (pt.at[c, xm, k, top], rxf.at[c, 1, k])
            send(c, then, [right, left], x_to)

    def groups_of(c):
        return list(zip(by_shard(c, 8), by_shard(c, 10)))

    def r1x(c):
        first_sum(c, groups_of(c))

    def r1x0(c):
        first_sum(c, groups_of(c)[:1])

    def r1x1(c):
        first_sum(c, groups_of(c)[1:3])

    def r1x2(c):
        first_sum(c, groups_of(c)[3:])

    def r1z(c):
        arrive(c, 9)
        for k in range(SIDE):
            add(c, k, zp, low_end, bzh[c, 0, k])
            add(c, k, zm, high_end, bzh[c, 1, k])
        send(
            c,
            11,
            [
                (pt.at[c, every, zp, end], bzf.at[c, 0]),
                (pt.at[c, every, zm, end], bzf.at[c, 1]),
            ],
            z_to,
        )

    def second_sum(c, groups):
        for phase, k in groups:
            arrive(c, phase)
            for j in range(SIDE) if k is every else (k,):
                add(c, x, j, top, rxf[c, 0, j], rxf[c, 1, j])

    def send_far(c):
        low = (pt.at[c, x, z2, low_half], rzh.at[c, 0])
        high = (pt.at[c, x, z2, high_half], rzh.at[c, 1])
        send(c, 12, [low, high], z_to)

    def r2z(c):
        second_sum(c, by_shard(c, 10))
        send_far(c)

    def r2z0(c):
        second_sum(c, by_shard(c, 10)[:1])
        send_far(c)

    def r2z1(c):
        second_sum(c, by_shard(c, 10)[1:3])

    def r2z2(c):
        second_sum(c, by_shard(c, 10)[3:])

    def r2x(c):
        arrive(c, 11)
        for k in range(SIDE):
            add(c, k, z, end, bzf[c, 0, k], bzf[c, 1, k])
        send(
            c,
            13,
            [
                (pt.at[c, x2, z, low_end], bxh.at[c, 0]),
                (pt.at[c, x2, z, high_end], bxh.at[c, 1]),
            ],
            x_to,
        )

    def r3z(c):
        arrive(c, 12)
        add(c, x, zp, low_half, rzh[c, 0])
        add(c, x, zm, high_half, rzh[c, 1])
        send(
            c,
            14,
            [(pt.at[c, x, zp, top], rzf.at[c, 0]), (pt.at[c, x, zm, top], rzf.at[c, 1])],
            z_to,
        )

    def r3x(c):
        arrive(c, 13)
        add(c, xp, z, low_end, bxh[c, 0])
        add(c, xm, z, high_end, bxh[c, 1])
        send(
            c,
            15,
            [(pt.at[c, xp, z, end], bxf.at[c, 0]), (pt.at[c, xm, z, end], bxf.at[c, 1])],
            x_to,
        )

    frag = frag_ref[0]
    index = lax.bitwise_and(frag, FRAGS - 1)
    rate = 0.4 + 0.6 * frag.astype(F32) / WINDOWS
    width = cw * nc // FRAGS

    def r4(c):
        chosen = index == (c * cw) // width
        inside = pl.ds((c * cw) % width, cw)
        for phase, part, far in ((14, top, rzf), (15, end, bxf)):
            arrive(c, phase)
            grad = pt[c, x, z, part, :].astype(F32)
            grad = (grad + far[c, 0].astype(F32) + far[c, 1].astype(F32)) * scale
            old = w[part, cols(c)]
            moment1 = 0.9 * m1[part, cols(c)] + 0.1 * grad
            moment2 = 0.95 * m2[part, cols(c)] + 0.05 * grad * grad
            stepped = old - 0.25 * (moment1 / (jnp.sqrt(moment2) + 1e-08) + 0.1 * old)
            mixed = 0.5 * anc_full[part, inside] + 0.5 * stepped
            nw[part, cols(c)] = jnp.where(chosen, mixed, stepped)
        copy = pltpu.make_async_copy(nw.at[:, cols(c)], nw_hbm.at[:, cols(c)], out_sem.at[c])
        copy.start()
        sent["out", c] = copy

    spans = []
    base = 0
    share = width // replicas
    for k, h in enumerate(halves):
        size = width >> (k + 1)
        spans.append((base, base + h * size, base + (1 - h) * size, size))
        base = base + h * size
    own_rows = pl.ds(pl.multiple_of(base, share), share)

    def trade(k, n, src, dst):
        copy = pltpu.make_async_remote_copy(
            src_ref=src,
            dst_ref=dst,
            send_sem=osend.at[n],
            recv_sem=orecv.at[n],
            device_id={"replica": partners[k]},
            device_id_type=MESH,
        )
        copy.start()
        sent["outer", n] = copy

    def halve(k):
        _, keep, give, size = spans[k]
        trade(
            k,
            k,
            old_t.at[pl.ds(pl.multiple_of(give, share), size)],
            got.at[pl.ds(size, size)],
        )

    def halve_done(k):
        _, keep, give, size = spans[k]
        sent["outer", k].wait_recv()
        kept = pl.ds(pl.multiple_of(keep, share), size)
        old_t[kept, :] = old_t[kept, :] + got[pl.ds(size, size), :]

    def double(k):
        _, keep, give, size = spans[k]
        part = anc_t.at[pl.ds(pl.multiple_of(keep, share), size)]
        trade(k, len(bits) + k, part, part)

    def outer_begin():
        picked = w[:, pl.ds(0, width)]
        for k in range(1, FRAGS):
            picked = jnp.where(index == k, w[:, pl.ds(k * width, width)], picked)
        tall[pl.ds(0, rows), :] = picked
        tall[pl.ds(rows, LANES - rows), :] = jnp.zeros((LANES - rows, width), F32)
        anc_t[...] = tall[...].T
        for r in range(replicas):
            at = pl.ds(place(r, replicas) * share, share)
            old_t[at, :] = anc_t[pl.ds(r * share, share), :]
        halve(0)

    def outer_update():
        mean = old_t[own_rows, pl.ds(0, rows)] / replicas
        anchor, moment = anc_ref[0], mom_ref[0]
        for k in range(1, FRAGS):
            anchor = jnp.where(index == k, anc_ref[k], anchor)
            moment = jnp.where(index == k, mom_ref[k], moment)
        outer = anchor - mean
        moment = 0.9 * moment + outer
        anchor = anchor - rate * (outer + 0.9 * moment)
        for k in range(FRAGS):
            na_ref[k] = jnp.where(index == k, anchor, anc_ref[k])
            nm_ref[k] = jnp.where(index == k, moment, mom_ref[k])
        anc_t[own_rows, pl.ds(0, rows)] = anchor
        anc_t[own_rows, pl.ds(rows, LANES - rows)] = jnp.zeros((share, LANES - rows), F32)

    def outer_end():
        for r in range(replicas):
            at = pl.ds(place(r, replicas) * share, share)
            got[pl.ds(r * share, share), :] = anc_t[at, :]
        tall[...] = got[...].T
        anc_full[...] = tall[pl.ds(0, rows), :]

    def turn(k, count):
        tiles = depth // 128 // count

        def one(i, carry):
            at = pl.ds(pl.multiple_of((k * tiles + i) * 128, 128), 128)
            act_t[at, :] = act[:, at].T
            return carry

        lax.fori_loop(0, tiles, one, 0)

    steps = len(bits)
    outer = [outer_begin]
    for k in range(1, steps):
        outer.append(lambda k=k: (halve_done(k - 1), halve(k)))
    outer.append(lambda: (halve_done(steps - 1), outer_update(), double(steps - 1)))
    for k in range(steps - 1, 0, -1):
        outer.append(lambda k=k: (sent["outer", steps + k].wait_recv(), double(k - 1)))
    outer.append(lambda: (sent["outer", steps].wait_recv(), outer_end()))

    events = {
        "a0": a0,
        "a1z": a1z,
        "a1x": a1x,
        "a2x": a2x,
        "a2z": a2z,
        "a3x": a3x,
        "a3x0": a3x0,
        "a3x1": a3x1,
        "a3x2": a3x2,
        "a3z": a3z,
        "a4": a4,
        "C": compute,
        "r1x": r1x,
        "r1x0": r1x0,
        "r1x1": r1x1,
        "r1x2": r1x2,
        "r1z": r1z,
        "r2z": r2z,
        "r2z0": r2z0,
        "r2z1": r2z1,
        "r2z2": r2z2,
        "r2x": r2x,
        "r3z": r3z,
        "r3x": r3x,
        "r4": r4,
        "T": lambda c: turns.pop(0)(),
        "o": lambda c: outer.pop(0)(),
    }
    turns = [lambda: (loads[1].wait(), turn(0, 4)), lambda: turn(1, 4), lambda: turn(2, 4)]
    turns.append(lambda: (turn(3, 4), [load.wait() for load in loads[2:]]))
    loads[0].wait()
    pl.semaphore_wait(barrier, 4 + len(bits))
    for event, c in ORDER:
        events[event](c)
    for key, copies in sent.items():
        if key[0] == "out":
            copies.wait()
        elif key[0] == "outer":
            copies.wait_send()
        else:
            for copy in copies:
                copy.wait_send()


def shards(activations, teacher, weights, first_moment, second_moment, anchor, momentum, fragment):
    tokens, depth = activations.shape[1:]
    rows, width = weights.shape[1:]
    replicas = lax.axis_size("replica")
    share = anchor.shape[2]
    whole = share * replicas
    cw = width // CHUNKS
    ra, rb = ROWS_A, rows - ROWS_A
    batch = tokens * lax.axis_size("fsdp")
    bits = replicas.bit_length() - 1
    vmem = pltpu.VMEM
    anywhere = pl.BlockSpec(memory_space=pl.ANY)
    inside = pl.BlockSpec(memory_space=pltpu.VMEM)
    new_w, new_a, new_m = pl.pallas_call(
        functools.partial(kernel, batch),
        out_shape=(
            jax.ShapeDtypeStruct((rows, width), F32),
            jax.ShapeDtypeStruct((FRAGS, share, rows), F32),
            jax.ShapeDtypeStruct((FRAGS, share, rows), F32),
        ),
        in_specs=[pl.BlockSpec(memory_space=pltpu.SMEM)] + [anywhere] * 7,
        out_specs=(anywhere, inside, inside),
        scratch_shapes=[
            vmem((tokens, depth), BF16),
            vmem((depth, tokens), BF16),
            vmem((tokens, width), BF16),
            vmem((rows, width), F32),
            vmem((rows, width), F32),
            vmem((rows, width), F32),
            vmem((rows, width), F32),
            vmem((CHUNKS, SIDE, SIDE, rows, cw), BF16),
            vmem((CHUNKS, SIDE, SIDE, rows, cw), BF16),
            vmem((tokens, cw), BF16),
            vmem((CHUNKS, 2, SIDE, ra // 2, cw), BF16),
            vmem((CHUNKS, 2, SIDE, ra, cw), BF16),
            vmem((CHUNKS, 2, ra // 2, cw), BF16),
            vmem((CHUNKS, 2, ra, cw), BF16),
            vmem((CHUNKS, 2, SIDE, rb // 2, cw), BF16),
            vmem((CHUNKS, 2, SIDE, rb, cw), BF16),
            vmem((CHUNKS, 2, rb // 2, cw), BF16),
            vmem((CHUNKS, 2, rb, cw), BF16),
            vmem((FRAGS, share, rows), F32),
            vmem((FRAGS, share, rows), F32),
            vmem((LANES, whole), F32),
            vmem((whole, LANES), F32),
            vmem((whole, LANES), F32),
            vmem((rows, whole), F32),
            vmem((whole, LANES), F32),
            pltpu.SemaphoreType.DMA((7,)),
            pltpu.SemaphoreType.DMA((CHUNKS,)),
            pltpu.SemaphoreType.DMA((CHUNKS, PHASES, 2)),
            pltpu.SemaphoreType.DMA((CHUNKS, PHASES, 2)),
            pltpu.SemaphoreType.DMA((2 * bits,)),
            pltpu.SemaphoreType.DMA((2 * bits,)),
        ],
        compiler_params=pltpu.CompilerParams(
            collective_id=0, has_side_effects=True, vmem_limit_bytes=60 * 2**20
        ),
    )(
        fragment,
        activations[0],
        teacher[0],
        weights[0],
        first_moment[0],
        second_moment[0],
        jnp.swapaxes(anchor, 1, 2),
        jnp.swapaxes(momentum, 1, 2),
    )
    return (new_w[None], jnp.swapaxes(new_a, 1, 2), jnp.swapaxes(new_m, 1, 2))


def solution(mesh):
    in_specs = (
        P("replica", "fsdp", None),
        P("replica", "fsdp", None),
        P("replica", "fsdp", None),
        P("replica", "fsdp", None),
        P("replica", "fsdp", None),
        P(None, "fsdp", "replica"),
        P(None, "fsdp", "replica"),
        P(),
    )
    out_specs = (P("replica", "fsdp", None), P(None, "fsdp", "replica"), P(None, "fsdp", "replica"))
    return jax.shard_map(shards, mesh=mesh, in_specs=in_specs, out_specs=out_specs, check_vma=False)
```

```python
import functools
import math

import jax
import jax.numpy as jnp
from jax import lax
from jax.experimental import pallas as pl
from jax.experimental.pallas import tpu as pltpu
from jax.sharding import PartitionSpec as P

FRAGS = 4
WINDOWS = 256
SIDE = 4
CHUNKS = 4
ROWS_A = 224
LANES = 384
SPLIT_GATHER = (0, 1, 2)
SPLIT_SCATTER = (1, 2, 3)
ORDER = (
    ("a0", 0), ("a0", 2), ("a0", 1), ("a1x", 0), ("a1z", 0), ("a1x", 2), ("a1z", 2), ("a1z", 1), ("a1x", 1),
    ("a0", 3), ("T", 0), ("T", 0), ("a3x1", 0), ("a2x", 1), ("T", 0), ("a2x", 0), ("a2x", 2), ("a3x0", 0),
    ("a2z", 0), ("o", 0), ("a1z", 3), ("a3x0", 1), ("a2z", 1), ("a3x1", 1), ("a3x2", 0), ("a1x", 3),
    ("a3z", 0), ("a3z", 1), ("o", 0), ("a3x2", 2), ("a3x2", 1), ("a3x1", 2), ("T", 0), ("a2z", 2), ("o", 0),
    ("a3x0", 2), ("a2x", 3), ("a2z", 3), ("a4", 1), ("a4", 0), ("C", 0), ("a3z", 2), ("o", 0), ("C", 1),
    ("r1z", 0), ("r1x0", 1), ("a3x", 3), ("a4", 2), ("a3z", 3), ("C", 2), ("o", 0), ("r1x1", 1), ("r2z0", 1),
    ("r1z", 1), ("a4", 3), ("C", 3), ("r1x", 0), ("r1z", 2), ("r1x0", 2), ("r2z1", 1), ("r1x0", 3),
    ("r2x", 1), ("o", 0), ("r1x1", 3), ("r1z", 3), ("r3z", 1), ("o", 0), ("r2z0", 2), ("o", 0), ("r1x1", 2),
    ("r2z0", 3), ("r1x2", 1), ("r2x", 0), ("r2z", 0), ("r2z1", 3), ("r3z", 3), ("r2x", 2), ("r3z", 0),
    ("r2z1", 2), ("r1x2", 3), ("r3x", 0), ("r3z", 2), ("r2x", 3), ("r3x", 1), ("r2z2", 1), ("r1x2", 2),
    ("r3x", 3), ("r3x", 2), ("o", 0), ("r4", 0), ("r2z2", 3), ("r4", 1), ("r2z2", 2), ("r4", 3), ("r4", 2),
)
SHORT = (1, 3, 5, 7, 9, 11, 13, 15)
FULL = (0, 1, 4, 5, 10, 11, 14, 15, 16, 17, 18, 25, 26, 27)
KINDS = (0, 1, 0, 1, 2, 3, 2, 3, 4, 5, 4, 5, 6, 7, 6, 7) + (2,) * 6 + (4,) * 6
MESH = pl.DeviceIdType.MESH
F32 = jnp.float32
BF16 = jnp.bfloat16


def exchange_bits(replicas):
    bits = [1 << k for k in range(replicas.bit_length() - 1)]
    return bits[:1] + bits[2:] + bits[1:2]


def place(replica, replicas):
    at, size = 0, replicas // 2
    for bit in exchange_bits(replicas):
        at += size if replica & bit else 0
        size //= 2
    return at


def kernel(
    batch,
    frag_ref,
    act_hbm,
    tgt_hbm,
    w_hbm,
    m1_hbm,
    m2_hbm,
    anc_hbm,
    mom_hbm,
    nw_hbm,
    na_ref,
    nm_ref,
    act,
    act_t,
    tgt,
    w,
    m1,
    m2,
    nw,
    wf,
    pt,
    err,
    rxh,
    rxf,
    rzh,
    rzf,
    bzh,
    bzf,
    bxh,
    bxf,
    anc_ref,
    mom_ref,
    tall,
    old_t,
    anc_t,
    anc_full,
    got,
    in_sem,
    out_sem,
    ssem,
    rsem,
    osend,
    orecv,
):
    nc, rows, cw = wf.shape[0], wf.shape[3], wf.shape[4]
    ra, rb = ROWS_A, rows - ROWS_A
    ha, hb = ra // 2, rb // 2
    depth = act.shape[1]
    scale = 1.0 / math.sqrt(depth)
    group = SIDE * rows

    me = lax.axis_index("fsdp")
    rep = lax.axis_index("replica")
    replicas = lax.axis_size("replica")
    x, z = lax.div(me, SIDE), lax.rem(me, SIDE)
    xp, xm, x2 = (lax.rem(x + k, SIDE) for k in (1, 3, 2))
    zp, zm, z2 = (lax.rem(z + k, SIDE) for k in (1, 3, 2))
    x_to = [xp * SIDE + z, xm * SIDE + z]
    z_to = [x * SIDE + zp, x * SIDE + zm]
    bits = exchange_bits(replicas)
    halves = [lax.rem(lax.div(rep, b), 2) for b in bits]
    partners = [rep + b - 2 * b * h for b, h in zip(bits, halves)]

    barrier = pltpu.get_barrier_semaphore()
    for to in x_to + z_to:
        pl.semaphore_signal(barrier, inc=1, device_id={"fsdp": to}, device_id_type=MESH)
    for to in partners:
        pl.semaphore_signal(barrier, inc=1, device_id={"replica": to}, device_id_type=MESH)

    loads = [
        pltpu.make_async_copy(src, dst, in_sem.at[k])
        for k, (src, dst) in enumerate(
            [
                (w_hbm, w),
                (act_hbm, act),
                (tgt_hbm, tgt),
                (m1_hbm, m1),
                (m2_hbm, m2),
                (anc_hbm, anc_ref),
                (mom_hbm, mom_ref),
            ]
        )
    ]
    for load in loads:
        load.start()

    top, low_half, high_half = pl.ds(0, ra), pl.ds(0, ha), pl.ds(ha, ha)
    end, low_end, high_end = pl.ds(ra, rb), pl.ds(ra, hb), pl.ds(ra + hb, hb)
    every = pl.ds(0, SIDE)
    sent, others = {}, {}

    def send(c, phase, pairs, to):
        copies = []
        slot = sent.setdefault((c, phase), len(sent))
        for d in range(2):
            src, dst = pairs[d]
            copies.append(
                pltpu.make_async_remote_copy(
                    src_ref=src,
                    dst_ref=dst,
                    send_sem=ssem.at[KINDS[phase]],
                    recv_sem=rsem.at[slot],
                    device_id={"fsdp": to[d]},
                    device_id_type=MESH,
                )
            )
        for copy in copies:
            copy.start()

    def both(c, phase):
        part = end if phase in SHORT else top
        count = pl.ds(0, 2) if phase in FULL else 0
        wide = phase in (5, 7, 9, 11)
        wide = wide or (phase in (4, 6) and c not in SPLIT_GATHER)
        wide = wide or (phase in (8, 10) and c not in SPLIT_SCATTER)
        return wf.at[c, count, every, part] if wide else wf.at[c, 0, count, part]

    def arrive(c, phase):
        brought = both(c, phase)
        pltpu.make_async_copy(brought, brought, rsem.at[sent[c, phase]]).wait()

    def same(*refs):
        return [(r, r) for r in refs]

    def cols(c):
        return pl.ds(c * cw, cw)

    def a0(c):
        wf[c, x, z] = w[:, cols(c)].astype(BF16)
        own = wf.at[c, x, z, top]
        send(c, 0, same(own, own), z_to)
        short = wf.at[c, x, z, end]
        send(c, 1, same(short, short), x_to)
        if c in SPLIT_GATHER:
            send(c, 4, same(own, own), x_to)

    def a1z(c):
        arrive(c, 0)
        send(c, 2, same(wf.at[c, x, zm, low_half], wf.at[c, x, zp, high_half]), z_to)
        if c in SPLIT_GATHER:
            for phase, k in ((16, zm), (17, zp)):
                far = wf.at[c, x, k, top]
                send(c, phase, same(far, far), x_to)

    def a1x(c):
        arrive(c, 1)
        send(c, 3, same(wf.at[c, xm, z, low_end], wf.at[c, xp, z, high_end]), x_to)

    def a2x(c):
        arrive(c, 2)
        far = wf.at[c, x, z2, top] if c in SPLIT_GATHER else wf.at[c, x, every, top]
        send(c, 18 if c in SPLIT_GATHER else 4, same(far, far), x_to)

    def a2z(c):
        arrive(c, 3)
        own = wf.at[c, every, z, end]
        send(c, 5, same(own, own), z_to)

    def pass_on(c, phase, then, k):
        arrive(c, phase)
        send(c, then, same(wf.at[c, xm, k, low_half], wf.at[c, xp, k, high_half]), x_to)

    def a3x(c):
        pass_on(c, 4, 6, every)

    def a3x0(c):
        pass_on(c, 4, 6, z)

    def a3x1(c):
        pass_on(c, 16, 19, zm)
        pass_on(c, 17, 20, zp)

    def a3x2(c):
        pass_on(c, 18, 21, z2)

    def a3z(c):
        arrive(c, 5)
        send(c, 7, same(wf.at[c, every, zm, low_end], wf.at[c, every, zp, high_end]), z_to)

    def a4(c):
        for phase in (6, 19, 20, 21, 7) if c in SPLIT_GATHER else (6, 7):
            arrive(c, phase)

    def compute(c):
        total = None
        for g in range(SIDE):
            term = jnp.dot(
                act[:, pl.ds(g * group, group)],
                wf[c, g].reshape(group, cw),
                preferred_element_type=F32,
            )
            total = term if total is None else total + term
        values = total * scale
        err[...] = ((values - tgt[:, cols(c)].astype(F32)) / batch).astype(BF16)
        for g in (x2, xp, xm, x):
            part = jnp.dot(
                act_t[pl.ds(pl.multiple_of(g * group, group), group), :],
                err[...],
                preferred_element_type=F32,
            )
            pt[c, g] = part.astype(BF16).reshape(SIDE, rows, cw)
            if g is x2:
                for phase, k in by_shard(c, 8):
                    low = (pt.at[c, x2, k, low_half], rxh.at[c, 0, k])
                    high = (pt.at[c, x2, k, high_half], rxh.at[c, 1, k])
                    send(c, phase, [low, high], x_to)
        send(
            c,
            9,
            [
                (pt.at[c, every, z2, low_end], bzh.at[c, 0]),
                (pt.at[c, every, z2, high_end], bzh.at[c, 1]),
            ],
            z_to,
        )

    def by_shard(c, first):
        if c not in SPLIT_SCATTER:
            return [(first, every)]
        base = 22 if first == 8 else 25
        return [(first, z2), (base, zm), (base + 1, zp), (base + 2, z)]

    def add(c, i, j, part, *terms):
        total = pt[c, i, j, part, :].astype(F32)
        for term in terms:
            total = total + term.astype(F32)
        pt[c, i, j, part, :] = total.astype(BF16)

    def first_sum(c, groups):
        for (phase, k), (then, _) in groups:
            arrive(c, phase)
            for j in range(SIDE) if k is every else (k,):
                add(c, xp, j, low_half, rxh[c, 0, j])
                add(c, xm, j, high_half, rxh[c, 1, j])
            right = (pt.at[c, xp, k, top], rxf.at[c, 0, k])
            left = (pt.at[c, xm, k, top], rxf.at[c, 1, k])
            send(c, then, [right, left], x_to)

    def groups_of(c):
        return list(zip(by_shard(c, 8), by_shard(c, 10)))

    def r1x(c):
        first_sum(c, groups_of(c))

    def r1x0(c):
        first_sum(c, groups_of(c)[:1])

    def r1x1(c):
        first_sum(c, groups_of(c)[1:3])

    def r1x2(c):
        first_sum(c, groups_of(c)[3:])

    def r1z(c):
        arrive(c, 9)
        for k in range(SIDE):
            add(c, k, zp, low_end, bzh[c, 0, k])
            add(c, k, zm, high_end, bzh[c, 1, k])
        send(
            c,
            11,
            [
                (pt.at[c, every, zp, end], bzf.at[c, 0]),
                (pt.at[c, every, zm, end], bzf.at[c, 1]),
            ],
            z_to,
        )

    def second_sum(c, groups):
        for phase, k in groups:
            arrive(c, phase)
            for j in range(SIDE) if k is every else (k,):
                add(c, x, j, top, rxf[c, 0, j], rxf[c, 1, j])

    def send_far(c):
        low = (pt.at[c, x, z2, low_half], rzh.at[c, 0])
        high = (pt.at[c, x, z2, high_half], rzh.at[c, 1])
        send(c, 12, [low, high], z_to)

    def r2z(c):
        second_sum(c, by_shard(c, 10))
        send_far(c)

    def r2z0(c):
        second_sum(c, by_shard(c, 10)[:1])
        send_far(c)

    def r2z1(c):
        second_sum(c, by_shard(c, 10)[1:3])

    def r2z2(c):
        second_sum(c, by_shard(c, 10)[3:])

    def r2x(c):
        arrive(c, 11)
        for k in range(SIDE):
            add(c, k, z, end, bzf[c, 0, k], bzf[c, 1, k])
        send(
            c,
            13,
            [
                (pt.at[c, x2, z, low_end], bxh.at[c, 0]),
                (pt.at[c, x2, z, high_end], bxh.at[c, 1]),
            ],
            x_to,
        )

    def r3z(c):
        arrive(c, 12)
        add(c, x, zp, low_half, rzh[c, 0])
        add(c, x, zm, high_half, rzh[c, 1])
        send(
            c,
            14,
            [(pt.at[c, x, zp, top], rzf.at[c, 0]), (pt.at[c, x, zm, top], rzf.at[c, 1])],
            z_to,
        )

    def r3x(c):
        arrive(c, 13)
        add(c, xp, z, low_end, bxh[c, 0])
        add(c, xm, z, high_end, bxh[c, 1])
        send(
            c,
            15,
            [(pt.at[c, xp, z, end], bxf.at[c, 0]), (pt.at[c, xm, z, end], bxf.at[c, 1])],
            x_to,
        )

    frag = frag_ref[0]
    index = lax.bitwise_and(frag, FRAGS - 1)
    rate = 0.4 + 0.6 * frag.astype(F32) / WINDOWS
    width = cw * nc // FRAGS

    def r4(c):
        chosen = index == (c * cw) // width
        inside = pl.ds((c * cw) % width, cw)
        for phase, part, far in ((14, top, rzf), (15, end, bxf)):
            arrive(c, phase)
            grad = pt[c, x, z, part, :].astype(F32)
            grad = (grad + far[c, 0].astype(F32) + far[c, 1].astype(F32)) * scale
            old = w[part, cols(c)]
            moment1 = 0.9 * m1[part, cols(c)] + 0.1 * grad
            moment2 = 0.95 * m2[part, cols(c)] + 0.05 * grad * grad
            stepped = old - 0.25 * (moment1 / (jnp.sqrt(moment2) + 1e-08) + 0.1 * old)
            mixed = 0.5 * anc_full[part, inside] + 0.5 * stepped
            nw[part, cols(c)] = jnp.where(chosen, mixed, stepped)
        copy = pltpu.make_async_copy(nw.at[:, cols(c)], nw_hbm.at[:, cols(c)], out_sem.at[c])
        copy.start()
        others["out", c] = copy

    spans = []
    base = 0
    share = width // replicas
    for k, h in enumerate(halves):
        size = width >> (k + 1)
        spans.append((base, base + h * size, base + (1 - h) * size, size))
        base = base + h * size
    own_rows = pl.ds(pl.multiple_of(base, share), share)

    def trade(k, n, src, dst):
        copy = pltpu.make_async_remote_copy(
            src_ref=src,
            dst_ref=dst,
            send_sem=osend.at[n],
            recv_sem=orecv.at[n],
            device_id={"replica": partners[k]},
            device_id_type=MESH,
        )
        copy.start()
        others["outer", n] = copy

    def halve(k):
        _, keep, give, size = spans[k]
        trade(
            k,
            k,
            old_t.at[pl.ds(pl.multiple_of(give, share), size)],
            got.at[pl.ds(size, size)],
        )

    def halve_done(k):
        _, keep, give, size = spans[k]
        others["outer", k].wait_recv()
        kept = pl.ds(pl.multiple_of(keep, share), size)
        old_t[kept, :] = old_t[kept, :] + got[pl.ds(size, size), :]

    def double(k):
        _, keep, give, size = spans[k]
        part = anc_t.at[pl.ds(pl.multiple_of(keep, share), size)]
        trade(k, len(bits) + k, part, part)

    def outer_begin():
        picked = w[:, pl.ds(0, width)]
        for k in range(1, FRAGS):
            picked = jnp.where(index == k, w[:, pl.ds(k * width, width)], picked)
        tall[pl.ds(0, rows), :] = picked
        tall[pl.ds(rows, LANES - rows), :] = jnp.zeros((LANES - rows, width), F32)
        anc_t[...] = tall[...].T
        for r in range(replicas):
            at = pl.ds(place(r, replicas) * share, share)
            old_t[at, :] = anc_t[pl.ds(r * share, share), :]
        halve(0)

    def outer_update():
        mean = old_t[own_rows, pl.ds(0, rows)] / replicas
        anchor, moment = anc_ref[0], mom_ref[0]
        for k in range(1, FRAGS):
            anchor = jnp.where(index == k, anc_ref[k], anchor)
            moment = jnp.where(index == k, mom_ref[k], moment)
        outer = anchor - mean
        moment = 0.9 * moment + outer
        anchor = anchor - rate * (outer + 0.9 * moment)
        for k in range(FRAGS):
            na_ref[k] = jnp.where(index == k, anchor, anc_ref[k])
            nm_ref[k] = jnp.where(index == k, moment, mom_ref[k])
        anc_t[own_rows, pl.ds(0, rows)] = anchor
        anc_t[own_rows, pl.ds(rows, LANES - rows)] = jnp.zeros((share, LANES - rows), F32)

    def outer_end():
        for r in range(replicas):
            at = pl.ds(place(r, replicas) * share, share)
            got[pl.ds(r * share, share), :] = anc_t[at, :]
        tall[...] = got[...].T
        anc_full[...] = tall[pl.ds(0, rows), :]

    def turn(k, count):
        tiles = depth // 128 // count

        def one(i, carry):
            at = pl.ds(pl.multiple_of((k * tiles + i) * 128, 128), 128)
            act_t[at, :] = act[:, at].T
            return carry

        lax.fori_loop(0, tiles, one, 0)

    steps = len(bits)
    outer = [outer_begin]
    for k in range(1, steps):
        outer.append(lambda k=k: (halve_done(k - 1), halve(k)))
    outer.append(lambda: (halve_done(steps - 1), outer_update(), double(steps - 1)))
    for k in range(steps - 1, 0, -1):
        outer.append(lambda k=k: (others["outer", steps + k].wait_recv(), double(k - 1)))
    outer.append(lambda: (others["outer", steps].wait_recv(), outer_end()))

    events = {
        "a0": a0,
        "a1z": a1z,
        "a1x": a1x,
        "a2x": a2x,
        "a2z": a2z,
        "a3x": a3x,
        "a3x0": a3x0,
        "a3x1": a3x1,
        "a3x2": a3x2,
        "a3z": a3z,
        "a4": a4,
        "C": compute,
        "r1x": r1x,
        "r1x0": r1x0,
        "r1x1": r1x1,
        "r1x2": r1x2,
        "r1z": r1z,
        "r2z": r2z,
        "r2z0": r2z0,
        "r2z1": r2z1,
        "r2z2": r2z2,
        "r2x": r2x,
        "r3z": r3z,
        "r3x": r3x,
        "r4": r4,
        "T": lambda c: turns.pop(0)(),
        "o": lambda c: outer.pop(0)(),
    }
    turns = [lambda: (loads[1].wait(), turn(0, 4)), lambda: turn(1, 4), lambda: turn(2, 4)]
    turns.append(lambda: (turn(3, 4), [load.wait() for load in loads[2:]]))
    loads[0].wait()
    pl.semaphore_wait(barrier, 4 + len(bits))
    for event, c in ORDER:
        events[event](c)
    for (key, _), copy in others.items():
        if key == "out":
            copy.wait()
        else:
            copy.wait_send()
    chunks, three = pl.ds(0, nc), pl.ds(0, 3)
    narrow, wide = wf.at[chunks, 0, three], wf.at[chunks, three]
    for kind, (block, part) in enumerate(
        [(narrow, top), (narrow, end), (wide, top), (wide, end)]
        + [(wide, top), (wide, end), (narrow, top), (narrow, end)]
    ):
        gone = block.at[:, :, :, part] if block is wide else block.at[:, :, part]
        pltpu.make_async_copy(gone, gone, ssem.at[kind]).wait()


def shards(activations, teacher, weights, first_moment, second_moment, anchor, momentum, fragment):
    tokens, depth = activations.shape[1:]
    rows, width = weights.shape[1:]
    replicas = lax.axis_size("replica")
    share = anchor.shape[2]
    whole = share * replicas
    cw = width // CHUNKS
    ra, rb = ROWS_A, rows - ROWS_A
    batch = tokens * lax.axis_size("fsdp")
    bits = replicas.bit_length() - 1
    slots = CHUNKS * 16 + 6 * (len(SPLIT_GATHER) + len(SPLIT_SCATTER))
    vmem = pltpu.VMEM
    anywhere = pl.BlockSpec(memory_space=pl.ANY)
    inside = pl.BlockSpec(memory_space=pltpu.VMEM)
    new_w, new_a, new_m = pl.pallas_call(
        functools.partial(kernel, batch),
        out_shape=(
            jax.ShapeDtypeStruct((rows, width), F32),
            jax.ShapeDtypeStruct((FRAGS, share, rows), F32),
            jax.ShapeDtypeStruct((FRAGS, share, rows), F32),
        ),
        in_specs=[pl.BlockSpec(memory_space=pltpu.SMEM)] + [anywhere] * 7,
        out_specs=(anywhere, inside, inside),
        scratch_shapes=[
            vmem((tokens, depth), BF16),
            vmem((depth, tokens), BF16),
            vmem((tokens, width), BF16),
            vmem((rows, width), F32),
            vmem((rows, width), F32),
            vmem((rows, width), F32),
            vmem((rows, width), F32),
            vmem((CHUNKS, SIDE, SIDE, rows, cw), BF16),
            vmem((CHUNKS, SIDE, SIDE, rows, cw), BF16),
            vmem((tokens, cw), BF16),
            vmem((CHUNKS, 2, SIDE, ra // 2, cw), BF16),
            vmem((CHUNKS, 2, SIDE, ra, cw), BF16),
            vmem((CHUNKS, 2, ra // 2, cw), BF16),
            vmem((CHUNKS, 2, ra, cw), BF16),
            vmem((CHUNKS, 2, SIDE, rb // 2, cw), BF16),
            vmem((CHUNKS, 2, SIDE, rb, cw), BF16),
            vmem((CHUNKS, 2, rb // 2, cw), BF16),
            vmem((CHUNKS, 2, rb, cw), BF16),
            vmem((FRAGS, share, rows), F32),
            vmem((FRAGS, share, rows), F32),
            vmem((LANES, whole), F32),
            vmem((whole, LANES), F32),
            vmem((whole, LANES), F32),
            vmem((rows, whole), F32),
            vmem((whole, LANES), F32),
            pltpu.SemaphoreType.DMA((7,)),
            pltpu.SemaphoreType.DMA((CHUNKS,)),
            pltpu.SemaphoreType.DMA((8,)),
            pltpu.SemaphoreType.DMA((slots,)),
            pltpu.SemaphoreType.DMA((2 * bits,)),
            pltpu.SemaphoreType.DMA((2 * bits,)),
        ],
        compiler_params=pltpu.CompilerParams(
            collective_id=0, has_side_effects=True, vmem_limit_bytes=60 * 2**20
        ),
    )(
        fragment,
        activations[0],
        teacher[0],
        weights[0],
        first_moment[0],
        second_moment[0],
        jnp.swapaxes(anchor, 1, 2),
        jnp.swapaxes(momentum, 1, 2),
    )
    return (new_w[None], jnp.swapaxes(new_a, 1, 2), jnp.swapaxes(new_m, 1, 2))


def solution(mesh):
    in_specs = (
        P("replica", "fsdp", None),
        P("replica", "fsdp", None),
        P("replica", "fsdp", None),
        P("replica", "fsdp", None),
        P("replica", "fsdp", None),
        P(None, "fsdp", "replica"),
        P(None, "fsdp", "replica"),
        P(),
    )
    out_specs = (P("replica", "fsdp", None), P(None, "fsdp", "replica"), P(None, "fsdp", "replica"))
    return jax.shard_map(shards, mesh=mesh, in_specs=in_specs, out_specs=out_specs, check_vma=False)
```
